32 devices in a mesh: row: 8 (over y, x, core), col: 4 (over z).
Axes of the slice: x: 2, y: 2, z: 4, core: 2. Of those that a mesh axis runs over, the one named last changes fastest.
Arguments:
- matrix: float32 [256, 64, 8, 2048], P(None, 'row', None, 'col'), as said below
Outputs:
- factored: float32 [256, 64, 8, 2048], P(None, 'row', None, 'col')
Inputs may be any that keep to these rules, and one draw needn't show every extreme that they name: `matrix`: symmetric and positive definite.
All inputs are finite; a program needn't handle non-finite values.
Results may differ from the reference program's by a relative error of at most 0.0003.
Values sent between devices are 32-bit elements; how exact they have to be, the bound alone decides.
A program may use at most 256 MiB of HBM per device.

```python
import math
import jax
import jax.numpy as jnp
from jax import lax

ORDER = 16384
CB = 512
RB = 8
PANELS = 2
LR = 256
LC = 8
N_ROW = 8
N_COL = 4


def draw_matrix(key, part):
    key_lower, key_diag, key_tail, key_noise, key_shift = jax.random.split(key, 5)
    matrix_order = ORDER
    lead_count = PANELS * CB
    rest_count = matrix_order - lead_count
    lower_raw = jax.random.normal(key_lower, (lead_count, lead_count), jnp.float32)
    tail_rows = jax.random.normal(key_tail, (rest_count, lead_count), jnp.float32)
    noise_draw = jax.random.normal(key_noise, (rest_count, rest_count), jnp.float32)
    diag_factor = jax.random.uniform(key_diag, (lead_count,), jnp.float32, 1.0, 2.0)
    lead_factor = jnp.tril(lower_raw, -1) * (0.4 / math.sqrt(lead_count)) + jnp.diag(diag_factor)
    stacked_factor = jnp.concatenate([lead_factor, tail_rows], axis=0)
    product = jnp.dot(stacked_factor, stacked_factor.T, precision=lax.Precision.HIGHEST, preferred_element_type=jnp.float32)
    product = (product + product.T) * 0.5
    sym_noise = (noise_draw + noise_draw.T) * (0.70710678 * 0.1)
    shift_values = 0.1 * math.sqrt(rest_count) * jax.random.uniform(key_shift, (rest_count,), jnp.float32, 2.5, 4.0)
    positions = jnp.arange(rest_count)
    sym_noise = sym_noise.at[positions, positions].set(shift_values)
    tail_block = product[lead_count:, lead_count:] + sym_noise
    assembled = product.at[lead_count:, lead_count:].set(tail_block)
    return assembled.reshape(LR, N_ROW * RB, LC, N_COL * CB)


def setup_inputs(seed: int = 0) -> dict:
    splits = jax.random.split(jax.random.key(seed), 2)
    matrix = draw_matrix(jax.random.fold_in(splits[1], 71), 0)
    return dict(matrix=matrix)


def reference(matrix):
    matrix_order = ORDER
    factored_count = PANELS * CB
    highest = lax.Precision.HIGHEST
    working = matrix.reshape(matrix_order, matrix_order)
    factor_columns = []
    for panel_number in range(PANELS):
        start_col = panel_number * CB
        stop_col = start_col + CB
        factor_block = jnp.linalg.cholesky(working[start_col:stop_col, start_col:stop_col])
        below_rows = jax.scipy.linalg.solve_triangular(factor_block, working[stop_col:, start_col:stop_col].T, lower=True).T
        product = jnp.dot(below_rows.astype(jnp.float32), below_rows.T.astype(jnp.float32), precision=highest, preferred_element_type=jnp.float32)
        working = working.at[stop_col:, stop_col:].set(working[stop_col:, stop_col:] - product)
        factor_column = jnp.concatenate([jnp.zeros((start_col, CB), jnp.float32), factor_block, below_rows], axis=0)
        factor_columns.append(factor_column)
    left_part = jnp.concatenate(factor_columns, axis=1)
    right_part = jnp.concatenate([jnp.zeros((factored_count, matrix_order - factored_count), jnp.float32), working[factored_count:, factored_count:]], axis=0)
    assembled = jnp.concatenate([left_part, right_part], axis=1)
    return assembled.reshape(LR, N_ROW * RB, LC, N_COL * CB)
```

```python
import functools

import jax
import jax.numpy as jnp
from jax import lax
from jax.experimental import pallas as pl
from jax.experimental.pallas import tpu as pltpu
from jax.sharding import PartitionSpec as P

PANELS = 2
BLOCK = 128
MIB = 2**20
HIGHEST = lax.Precision.HIGHEST


def dot(a, b, dims=((1,), (0,)), precision=HIGHEST):
    return lax.dot_general(
        a, b, (dims, ((), ())), precision=precision, preferred_element_type=jnp.float32
    )


def eliminate(diag):
    size = diag.shape[0]
    lane = lax.broadcasted_iota(jnp.int32, (8, size), 1)
    sub = lax.broadcasted_iota(jnp.int32, (8, size), 0)
    parts = [diag[8 * i : 8 * i + 8, :] for i in range(size // 8)]
    for j in range(size):
        b, s = divmod(j, 8)
        row = parts[b][s : s + 1, :]
        inverse = 1.0 / row[:, j : j + 1]
        row = jnp.where(lane[:1] == j, 1.0, row) * inverse
        here = lane == j
        for i in range(b, size // 8):
            if i == b and s == 7:
                continue
            scale = parts[i][:, j : j + 1]
            if i == b:
                below = sub > s
                base = jnp.where(here & below, 0.0, parts[i])
                parts[i] = base - jnp.where(below, scale * row, 0.0)
            else:
                parts[i] = jnp.where(here, 0.0, parts[i]) - scale * row
    return jnp.concatenate(parts, axis=0)


def cholesky_kernel(s_ref, f_ref, inv_ref):
    order = s_ref.shape[0]
    steps = order // BLOCK
    inv_ref[...] = s_ref[...]
    rows_i = lax.broadcasted_iota(jnp.int32, (BLOCK, BLOCK), 0)
    cols_i = lax.broadcasted_iota(jnp.int32, (BLOCK, BLOCK), 1)

    @pl.loop(0, steps)
    def _(k):
        at_k = pl.ds(pl.multiple_of(k * BLOCK, BLOCK), BLOCK)
        work = eliminate(inv_ref[at_k, at_k])
        pivot = jnp.sum(jnp.where(rows_i == cols_i, work, 0.0), axis=1, keepdims=True)
        root = lax.rsqrt(pivot)
        root = root * (1.5 - 0.5 * pivot * root * root)
        upper = jnp.where(cols_i >= rows_i, work, 0.0) * root
        low_inv = jnp.where(
            cols_i < rows_i, work, jnp.where(cols_i == rows_i, 1.0, 0.0)
        ) * root
        full = dot(low_inv, inv_ref[at_k, :])
        inv_ref[at_k, :] = full
        inv_ref[at_k, at_k] = low_inv
        f_ref[:, at_k] = jnp.zeros((order, BLOCK), jnp.float32)
        f_ref[at_k, at_k] = upper.T

        @pl.loop(k + 1, steps)
        def _(i):
            at_i = pl.ds(pl.multiple_of(i * BLOCK, BLOCK), BLOCK)
            low = dot(inv_ref[at_i, at_k], low_inv, ((1,), (1,)))
            f_ref[at_i, at_k] = low
            inv_ref[at_i, at_k] = jnp.zeros((BLOCK, BLOCK), jnp.float32)
            inv_ref[at_i, :] -= dot(low, inv_ref[at_k, :])

    @pl.loop(0, steps)
    def _(k):
        for j in range(steps):
            at_j = pl.ds(j * BLOCK, BLOCK)

            @pl.when(j > k)
            def _():
                at_k = pl.ds(pl.multiple_of(k * BLOCK, BLOCK), BLOCK)
                inv_ref[at_k, at_j] = jnp.zeros((BLOCK, BLOCK), jnp.float32)


def cholesky(lead):
    order = lead.shape[0]
    shape = jax.ShapeDtypeStruct((order, order), jnp.float32)
    return pl.pallas_call(
        cholesky_kernel,
        out_shape=(shape, shape),
        in_specs=[pl.BlockSpec(memory_space=pltpu.VMEM)],
        out_specs=[pl.BlockSpec(memory_space=pltpu.VMEM)] * 2,
        compiler_params=pltpu.CompilerParams(vmem_limit_bytes=40 * MIB),
        cost_estimate=pl.CostEstimate(
            flops=100_000_000_000, bytes_accessed=12 * MIB, transcendentals=0
        ),
        name="cholesky",
    )(lead)


def pick_kernel(row_devices, in_ref, out_ref):
    slots, picked, _ = out_ref.shape
    width = in_ref.shape[2]
    index = lax.broadcasted_iota(jnp.int32, (picked, width), 0)
    column = lax.broadcasted_iota(jnp.int32, (picked, width), 1)
    wanted = (index // 8 * row_devices + lax.axis_index("row")) * 8 + index % 8
    select = jnp.where(column == wanted, 1.0, 0.0)
    for m in range(slots):
        out_ref[m] = dot(select, in_ref[:, m, :], ((1,), (1,)))


def pick(gathered, row_devices):
    order, slots, width = gathered.shape
    chunk = 256
    return pl.pallas_call(
        functools.partial(pick_kernel, row_devices),
        grid=(order // chunk,),
        out_shape=jax.ShapeDtypeStruct((slots, width // row_devices, order), jnp.float32),
        in_specs=[pl.BlockSpec((chunk, slots, width), lambda i: (i, 0, 0))],
        out_specs=pl.BlockSpec((slots, width // row_devices, chunk), lambda i: (0, 0, i)),
        compiler_params=pltpu.CompilerParams(vmem_limit_bytes=40 * MIB),
        name="pick",
    )(gathered)


def split(x):
    high = x.astype(jnp.bfloat16)
    return high, (x - high.astype(jnp.float32)).astype(jnp.bfloat16)


def columns_kernel(inv_ref, in_ref, high_ref, low_ref, last_ref):
    order, slots, _ = in_ref.shape
    step = 256
    for m in range(slots):
        raw = in_ref[:, m, :]
        for low in range(0, order, step):
            high = low + step
            solved = dot(inv_ref[low:high, :high], raw[:high])
            first, second = split(solved)
            rest = solved - first.astype(jnp.float32) - second.astype(jnp.float32)
            high_ref[m, low:high, :] = first
            low_ref[m, low:high, :] = second
            last_ref[m, low:high, :] = rest.astype(jnp.bfloat16)


def solve_columns(inverse, gathered):
    order, slots, width = gathered.shape
    chunk = 128
    shape = jax.ShapeDtypeStruct((slots, order, width), jnp.bfloat16)
    spec = pl.BlockSpec((slots, order, chunk), lambda i: (0, 0, i))
    return pl.pallas_call(
        columns_kernel,
        grid=(width // chunk,),
        out_shape=(shape, shape, shape),
        in_specs=[
            pl.BlockSpec((order, order), lambda i: (0, 0), pipeline_mode=pl.Buffered(1)),
            pl.BlockSpec((order, slots, chunk), lambda i: (0, 0, i)),
        ],
        out_specs=[spec, spec, spec],
        compiler_params=pltpu.CompilerParams(vmem_limit_bytes=56 * MIB),
        name="solve_columns",
    )(inverse, gathered)


def update_kernel(
    col_devices,
    rows_ref,
    inv_ref,
    own_ref,
    high_ref,
    low_ref,
    last_ref,
    in_ref,
    out_ref,
    solved_ref,
):
    blocks, row_block, slots, width = in_ref.shape
    rows, order = rows_ref.shape
    step = 256
    col = lax.axis_index("col")
    first = pl.program_id(0) == 0

    @pl.when(first)
    def _():
        out_ref[...] = jnp.zeros(out_ref.shape, jnp.float32)
        for p in range(PANELS):

            @pl.when(col == p % col_devices)
            def _():
                own = own_ref[:, p * width : (p + 1) * width]
                out_ref[:, :, p // col_devices, :] = own.reshape(blocks, row_block, width)

    @pl.when(jnp.logical_not(first))
    def _():
        for low in range(0, order, step):
            high = low + step
            solved_ref[:, low:high] = dot(
                rows_ref[:, :high], inv_ref[low:high, :high], ((1,), (1,))
            )
        high_rows, low_rows = split(solved_ref[...])
        for m in range(slots):
            product = dot(high_rows, last_ref[m], precision=None)
            product += dot(low_rows, low_ref[m], precision=None)
            product += dot(high_rows, low_ref[m], precision=None)
            product += dot(low_rows, high_ref[m], precision=None)
            product += dot(high_rows, high_ref[m], precision=None)
            out_ref[:, :, m, :] = in_ref[:, :, m, :] - product.reshape(
                blocks, row_block, width
            )
        for p in range(PANELS):

            @pl.when(col == p % col_devices)
            def _():
                own = solved_ref[:, p * width : (p + 1) * width]
                out_ref[:, :, p // col_devices, :] = own.reshape(blocks, row_block, width)


def update(rows, inverse, own, columns, matrix, col_devices):
    block_count, row_block, slots, width = matrix.shape
    lead_rows, order = own.shape
    lead_blocks = lead_rows // row_block
    once = pl.Buffered(1)
    return pl.pallas_call(
        functools.partial(update_kernel, col_devices),
        grid=(block_count // lead_blocks,),
        out_shape=jax.ShapeDtypeStruct(matrix.shape, jnp.float32),
        in_specs=[
            pl.BlockSpec((lead_rows, order), lambda i: (i, 0)),
            pl.BlockSpec((order, order), lambda i: (0, 0), pipeline_mode=once),
            pl.BlockSpec((lead_rows, order), lambda i: (0, 0), pipeline_mode=once),
            *[pl.BlockSpec((slots, order, width), lambda i: (0, 0, 0), pipeline_mode=once)] * 3,
            pl.BlockSpec((lead_blocks, row_block, slots, width), lambda i: (i, 0, 0, 0)),
        ],
        out_specs=pl.BlockSpec((lead_blocks, row_block, slots, width), lambda i: (i, 0, 0, 0)),
        scratch_shapes=[pltpu.VMEM((lead_rows, order), jnp.float32)],
        compiler_params=pltpu.CompilerParams(vmem_limit_bytes=56 * MIB),
        name="update",
    )(rows, inverse, own, *columns, matrix)


def shards(matrix):
    block_count, row_block, slots, width = matrix.shape
    row_devices = lax.axis_size("row")
    col_devices = lax.axis_size("col")
    row_index = lax.axis_index("row")
    order = PANELS * width
    lead_blocks = order // (row_devices * row_block)
    top = matrix[:lead_blocks]
    used = (PANELS + col_devices - 1) // col_devices
    lead = lax.all_gather(top[:, :, :used, :], "col", axis=3)
    lead = lead.reshape(lead_blocks, 1, row_block, used * col_devices * width)[..., :order]
    lead = lax.all_gather(lead, "row", axis=1, tiled=True).reshape(order, order)
    gathered = lax.all_gather(top[:, None], "row", axis=1, tiled=True)
    gathered = gathered.reshape(order, slots, width)
    own_part = pick(gathered, row_devices)
    rows = lax.all_gather(own_part[:, None], "col", axis=1, tiled=True)
    rows = rows.reshape(block_count * row_block, order)
    factor, inverse = cholesky(lead)
    own = lax.dynamic_index_in_dim(
        factor.reshape(lead_blocks, row_devices, row_block, order), row_index, 1, keepdims=False
    ).reshape(lead_blocks * row_block, order)
    columns = solve_columns(inverse, gathered)
    return update(rows, inverse, own, columns, matrix, col_devices)


def solution(mesh):
    return jax.shard_map(
        shards,
        mesh=mesh,
        in_specs=(P(None, "row", None, "col"),),
        out_specs=P(None, "row", None, "col"),
        check_vma=False,
    )
```
